32 devices in a mesh: opair: 4 (over y, core), vpair: 8 (over z, x).
Axes of the slice: x: 2, y: 2, z: 4, core: 2. Of those that a mesh axis runs over, the one named last changes fastest.
Arguments:
- amplitudes: bfloat16 [800, 12, 1000], P('vpair', 'opair'), may hold values from -6 to 6
- ladder_ints: bfloat16 [12, 1000, 8, 1000], P('opair', None, 'vpair'), may hold values from -0.0546875 to 0.0546875
- cycle_amps: bfloat16 [12, 100, 64], P('opair'), may hold values from -6 to 6
- cycle_ints: bfloat16 [12, 100, 100000], P('opair', None, 'vpair'), may hold values from -0.1875 to 0.1875
- occ_blocks: int32 [8], replicated, may hold values from 1 to 33, 100 in all
- virt_blocks: int32 [8], replicated, may hold values from 1 to 250, 1000 in all
- occ_start: int32 [1], replicated, may hold values from 0 to 92
- virt_start: int32 [1], replicated, may hold values from 0 to 992
- eps_occ: float32 [100], replicated, may hold values from -1 to -0.25
- eps_virt: float32 [1000], replicated, may hold values from 0.25 to 1.5
Outputs:
- update: float32 [8, 8, 100, 1000], P('opair', 'vpair')
The draws below stay inside these ranges and needn't reach their ends.
All inputs are finite; a program needn't handle non-finite values.
Results may differ from the reference program's by a relative error of at most 0.0004.
Values may be sent and summed in bfloat16 or wider, within the bound.
A program may use at most 128 MiB of HBM per device.

```python
import math
import jax
import jax.numpy as jnp
import numpy as np
from jax import lax

NO = 100
NV = 1000
I_WIN = 8
A_WIN = 8
C_WIN = 12
PAIRS = 800


def level_of(own_key, shape, pieces, low, top_value):
    loudness = 1.0
    for axis_at, parts in pieces:
        draws = jax.random.uniform(jax.random.fold_in(jax.random.fold_in(own_key, 6), axis_at), (parts,), jnp.float32, low / len(pieces), top_value / len(pieces))
        loudness = loudness * jnp.repeat(jnp.exp(draws), shape[axis_at] // parts).reshape((-1,) + (1,) * (len(shape) - 1 - axis_at))
    return loudness


def split_up(amount, total, bound, lean):
    loads = [(1 << 20) // math.isqrt(standing ** lean) + 1 for standing in range(2, amount + 1)]
    rest, holding = total - bound - (amount - 1), [1] * (amount - 1)
    while rest > 0:
        movable = [i for i in range(amount - 1) if holding[i] < bound]
        pool, left = sum([loads[i] for i in movable]), rest
        for i in movable:
            more = min(bound - holding[i], max(1, left * loads[i] // pool), rest)
            holding[i] = holding[i] + more
            rest = rest - more
    return np.array([bound] + holding)


def ragged(own_key, number_of, total, bound, slope):
    if number_of == 2:
        one = jax.random.randint(own_key, (), max(1, total - bound), min(bound, total - 1) + 1)
        return jnp.stack([one, total - one])
    lengths = jnp.asarray(split_up(number_of, total, bound, slope), jnp.int32)
    couples = (number_of - 1) // 2
    giver, sink = lengths[1:1 + 2 * couples:2], lengths[2:2 + 2 * couples:2]
    margin = jnp.minimum(giver - 1, bound - sink)
    shifted = jax.random.randint(jax.random.fold_in(own_key, 1), (couples,), 0, 1 << 20) % (margin + 1)
    lengths = lengths.at[1:1 + 2 * couples:2].set(giver - shifted).at[2:2 + 2 * couples:2].set(sink + shifted)
    return lengths[jax.random.permutation(jax.random.fold_in(own_key, 2), number_of)]


def normal_values(key, extent, deviation, reach, cuts=(), kind=jnp.bfloat16):
    array = deviation * jax.random.normal(key, extent, jnp.float32)
    if cuts:
        array = array * level_of(key, extent, cuts, -0.22, 0.18)
    return jnp.clip(array, -reach, reach).astype(kind)


def setup_inputs(seed: int = 0) -> dict:
    splits = jax.random.split(jax.random.key(seed), 11)
    return {
        "amplitudes": normal_values(splits[0], (PAIRS, C_WIN, NV), 1.0, 6.0, ((0, 8), (1, 4))),
        "ladder_ints": normal_values(splits[1], (C_WIN, NV, A_WIN, NV), (C_WIN * NV) ** -0.5, 0.0546875, ((0, 4), (2, 8))),
        "cycle_amps": normal_values(splits[2], (C_WIN, NO, I_WIN * A_WIN), 1.0, 6.0, ((0, 4),)),
        "cycle_ints": normal_values(splits[3], (C_WIN, NO, NO * NV), (C_WIN * NO) ** -0.5, 0.1875, ((0, 4), (2, 8))),
        "occ_blocks": ragged(splits[4], 8, NO, NO // 3, 2).astype(jnp.int32),
        "virt_blocks": ragged(splits[5], 8, NV, NV // 4, 2).astype(jnp.int32),
        "occ_start": jax.random.randint(splits[6], (1,), 0, NO - I_WIN + 1).astype(jnp.int32),
        "virt_start": jax.random.randint(splits[7], (1,), 0, NV - A_WIN + 1).astype(jnp.int32),
        "eps_occ": jnp.clip(jax.random.uniform(splits[8], (NO,), jnp.float32, -1.0, -0.25), -1.0, -0.25),
        "eps_virt": jnp.clip(jax.random.uniform(splits[9], (NV,), jnp.float32, 0.25, 1.5), 0.25, 1.5),
    }


def irrep_of(blocks, index):
    bounds = jnp.cumsum(blocks)[:-1]
    return jnp.sum((index[:, None] >= bounds[None, :]).astype(jnp.int32), axis=1)


def reference(amplitudes, ladder_ints, cycle_amps, cycle_ints, occ_blocks, virt_blocks, occ_start, virt_start, eps_occ, eps_virt):
    def accumulate(carry, slab):
        ladder, cycle = carry
        t_slab = lax.dynamic_index_in_dim(amplitudes, slab, 1, keepdims=False)
        v_slab = lax.dynamic_index_in_dim(ladder_ints, slab, 0, keepdims=False).reshape(NV, A_WIN * NV)
        ladder = ladder + jnp.dot(t_slab, v_slab, preferred_element_type=jnp.float32)
        x_slab = lax.dynamic_index_in_dim(cycle_amps, slab, 0, keepdims=False)
        y_slab = lax.dynamic_index_in_dim(cycle_ints, slab, 0, keepdims=False)
        cycle = cycle + jnp.dot(x_slab.T, y_slab, preferred_element_type=jnp.float32)
        return (ladder, cycle), None

    start = (jnp.zeros((PAIRS, A_WIN * NV), jnp.float32), jnp.zeros((I_WIN * A_WIN, NO * NV), jnp.float32))
    (ladder, cycle), _ = lax.scan(accumulate, start, jnp.arange(C_WIN, dtype=jnp.int32))
    ladder = ladder.reshape(I_WIN, NO, A_WIN, NV).transpose(0, 2, 1, 3)
    resid = ladder + cycle.reshape(I_WIN, A_WIN, NO, NV)
    first_occ = occ_start[0].astype(jnp.int32)
    first_virt = virt_start[0].astype(jnp.int32)
    glob_i = first_occ + jnp.arange(I_WIN, dtype=jnp.int32)
    glob_a = first_virt + jnp.arange(A_WIN, dtype=jnp.int32)
    sym_i = irrep_of(occ_blocks, glob_i)
    sym_a = irrep_of(virt_blocks, glob_a)
    sym_j = irrep_of(occ_blocks, jnp.arange(NO, dtype=jnp.int32))
    sym_b = irrep_of(virt_blocks, jnp.arange(NV, dtype=jnp.int32))
    total_sym = jnp.bitwise_xor(jnp.bitwise_xor(sym_i[:, None, None, None], sym_a[None, :, None, None]), jnp.bitwise_xor(sym_j[None, None, :, None], sym_b[None, None, None, :]))
    e_i = lax.dynamic_slice_in_dim(eps_occ, first_occ, I_WIN)
    e_a = lax.dynamic_slice_in_dim(eps_virt, first_virt, A_WIN)
    denom = e_i[:, None, None, None] - e_a[None, :, None, None] + eps_occ[None, None, :, None] - eps_virt[None, None, None, :]
    return jnp.where(total_sym == 0, resid / denom, jnp.float32(0.0))
```

```python
import functools

import jax
import jax.numpy as jnp
from jax import lax
from jax.experimental import pallas as pl
from jax.experimental.pallas import tpu as pltpu
from jax.sharding import PartitionSpec as P

NO = 100
NV = 1000
I_DEV = 2
A_DEV = 1
NVP = 1024
Q = 8
FULL = 32000.0
MESH = pl.DeviceIdType.MESH


def up_to(n, m):
    return (n + m - 1) // m * m


def row_length(n_v):
    x = 1
    while (2 * x) * (2 * x) * 2 <= n_v and n_v % (2 * x) == 0:
        x *= 2
    return x


def exponent(x):
    top = jnp.max(jnp.max(jnp.abs(x), axis=1, keepdims=True), axis=0, keepdims=True)
    return jnp.floor(jnp.log(jnp.maximum(top, 1e-30)) * 1.4426950408889634) + 1.0


def code(x, e, is_scale):
    q = jnp.round(x * (FULL * jnp.exp2(-e)))
    return jnp.where(is_scale, e, q).astype(jnp.int32).astype(jnp.int16)


def decode(q, e):
    return q.astype(jnp.float32) * (jnp.exp2(e) * (1.0 / FULL))


def kernel(
    n_o, n_v, pairs, pairs_pad, depth, jb, jb_pad, ch, a_win,
    amps, ints, w_ref, cyc_ints, lad_out, cyc_out,
    gat, b_buf, y_buf, part, cs, cr, total, tile, asend, arecv, acc, ls, lr,
    copy_sem, a_recv, up_send, down_send, x_send, c_send, c_recv, t_send, t_recv, l_send, l_recv,
):
    o = lax.axis_index("opair")
    v = lax.axis_index("vpair")
    nx = row_length(n_v)
    nz = n_v // nx
    z, x = v // nx, v % nx
    rows = a_win * I_DEV
    per_owner = n_v // n_o

    b_copy = pltpu.make_async_copy(ints, b_buf, copy_sem.at[0])
    y_copy = pltpu.make_async_copy(cyc_ints, y_buf, copy_sem.at[1])
    own_copy = pltpu.make_async_copy(amps, gat.at[v], copy_sem.at[2])
    y_copy.start()
    own_copy.start()
    b_copy.start()

    barrier = pltpu.get_barrier_semaphore()
    for t in range(1, n_v):
        pl.semaphore_signal(barrier, inc=1, device_id=(o, (v + t) % n_v), device_id_type=MESH)
    for s in range(1, n_o):
        pl.semaphore_signal(barrier, inc=1, device_id=((o + s) % n_o, v), device_id_type=MESH)
    pl.semaphore_wait(barrier, n_v - 1 + n_o - 1)

    def hop(src, slot, c, send, to):
        return pltpu.make_async_remote_copy(
            src_ref=src, dst_ref=gat.at[slot, c], send_sem=send, recv_sem=a_recv.at[slot, c],
            device_id=(o, to), device_id_type=MESH,
        )

    def block_src(slot, c, own):
        return amps.at[c] if own else gat.at[slot, c]

    def up_hop(d, c):
        slot = (z - d) * nx + x
        return hop(block_src(slot, c, d == 0), slot, c, up_send.at[d, c], v + nx)

    def down_hop(d, c):
        slot = (z + d) * nx + x
        return hop(block_src(slot, c, d == 0), slot, c, down_send.at[d, c], v - nx)

    def x_hops(k, zb, c):
        slot = zb * nx + x
        return [
            hop(block_src(slot, c, k == 0), slot, c, x_send.at[k, t - 1, c], z * nx + (x + t) % nx)
            for t in range(1, nx)
        ]

    def arrived(slot, c):
        pltpu.make_async_remote_copy(
            src_ref=gat.at[slot, c], dst_ref=gat.at[slot, c], send_sem=copy_sem.at[0],
            recv_sem=a_recv.at[slot, c], device_id=(o, v), device_id_type=MESH,
        ).wait_recv()

    for c in range(depth):
        if nz > 1:
            @pl.when(z + 1 < nz)
            def _():
                up_hop(0, c).start()

            @pl.when(z >= 1)
            def _():
                down_hop(0, c).start()
        for h in x_hops(0, z, c):
            h.start()

    acc[...] = jnp.zeros_like(acc)
    part[:, jb_pad - 128:] = jnp.zeros((part.shape[0], 128), jnp.float32)
    y_copy.wait()
    step = 14 * 128
    for at in range(0, jb, step):
        end = min(at + step, jb)
        sum_c = None
        for c in range(depth):
            term = jnp.dot(w_ref[c], y_buf[c, :, at:end], preferred_element_type=jnp.float32)
            sum_c = term if sum_c is None else sum_c + term
        part[:, at:end] = sum_c

    is_scale_c = lax.broadcasted_iota(jnp.int32, (rows, jb_pad), 1) == jb_pad - 1

    def c_hop(s):
        return pltpu.make_async_remote_copy(
            src_ref=cs.at[s - 1], dst_ref=cr.at[s - 1], send_sem=c_send.at[s - 1],
            recv_sem=c_recv.at[s - 1], device_id=((o + s) % n_o, v), device_id_type=MESH,
        )

    for s in range(1, n_o):
        to = (o + s) % n_o
        block = part[pl.ds(pl.multiple_of(to * rows, rows), rows), :]
        cs[s - 1] = code(block, exponent(block), is_scale_c)
        c_hop(s).start()

    col = lax.broadcasted_iota(jnp.int32, (pairs_pad, NVP), 1)

    def l_hop(slot):
        owner = slot // per_owner
        return pltpu.make_async_remote_copy(
            src_ref=ls.at[slot], dst_ref=lr.at[o, slot % per_owner], send_sem=l_send.at[slot],
            recv_sem=l_recv.at[o, slot % per_owner], device_id=(owner, v), device_id_type=MESH,
        )

    def multiply(slot):
        for at in range(0, NV, 256):
            end = min(at + 256, NV)
            sum_c = None
            for c in range(depth):
                term = jnp.dot(gat[slot, c], b_buf[c, :, at:end], preferred_element_type=jnp.float32)
                sum_c = term if sum_c is None else sum_c + term
            acc[:, at:end] = sum_c

        @pl.when(slot // per_owner == o)
        def _():
            lad_out[slot % per_owner] = acc[...]

        @pl.when(slot // per_owner != o)
        def _():
            block = acc[...]
            ls[slot] = code(block, exponent(block), col >= NV)
            l_hop(slot).start()

    def take_row(zb):
        def one(t, _):
            slot = zb * nx + (x + t) % nx
            for c in range(depth):
                arrived(slot, c)
            multiply(slot)
            return 0

        lax.fori_loop(1, nx, one, 0)

    own_copy.wait()
    b_copy.wait()
    multiply(v)

    def t_hop(t):
        to = (v + t) % n_v
        return pltpu.make_async_remote_copy(
            src_ref=asend.at[to], dst_ref=arecv.at[v], send_sem=t_send.at[t - 1],
            recv_sem=t_recv.at[t - 1], device_id=(o, to), device_id_type=MESH,
        )

    def cycle_exchange():
        sum_o = part[pl.ds(pl.multiple_of(o * rows, rows), rows), :]
        for s in range(1, n_o):
            c_hop(s).wait_recv()
            got = cr[s - 1]
            e = got[rows - 1:rows, jb_pad - 128:].astype(jnp.float32)[:, 127:128]
            sum_o = sum_o + jnp.where(is_scale_c, 0.0, decode(got, e))
        total[:, 0:jb_pad] = sum_o
        total[:, jb_pad:] = jnp.zeros((rows, Q * ch - jb_pad), jnp.float32)
        spot = (lax.broadcasted_iota(jnp.int32, (I_DEV * Q, ch), 0) == I_DEV * Q - 1) & (
            lax.broadcasted_iota(jnp.int32, (I_DEV * Q, ch), 1) == ch - 1
        )

        def one(t, _):
            a = (v + t) % n_v
            for i in range(I_DEV):
                for q in range(Q):
                    tile[a, i * Q + q:i * Q + q + 1, :] = total[pl.ds(a * I_DEV + i, 1), q * ch:q * ch + ch]
            block = tile[a]
            asend[a] = code(block, exponent(block), spot)
            return 0

        lax.fori_loop(0, n_v, one, 0)
        for t in range(1, n_v):
            t_hop(t).start()

    for d in range(1, nz):
        for c in range(depth):
            @pl.when(z - d >= 0)
            def _():
                arrived((z - d) * nx + x, c)

                @pl.when(z + 1 < nz)
                def _():
                    up_hop(d, c).start()

                for h in x_hops(d, z - d, c):
                    h.start()

            @pl.when(z + d < nz)
            def _():
                arrived((z + d) * nx + x, c)

                @pl.when(z >= 1)
                def _():
                    down_hop(d, c).start()

                for h in x_hops(nz - 1 + d, z + d, c):
                    h.start()

        if d == min(2, nz - 1):
            cycle_exchange()
        if d == 1:
            take_row(z)
        else:
            @pl.when(z - (d - 1) >= 0)
            def _():
                take_row(z - (d - 1))

            @pl.when(z + (d - 1) < nz)
            def _():
                take_row(z + (d - 1))

        @pl.when(z - d >= 0)
        def _():
            multiply((z - d) * nx + x)

        @pl.when(z + d < nz)
        def _():
            multiply((z + d) * nx + x)

    @pl.when(z - (nz - 1) >= 0)
    def _():
        take_row(z - (nz - 1))

    @pl.when(z + (nz - 1) < nz)
    def _():
        take_row(z + (nz - 1))

    cyc_out[v] = tile[v]
    for t in range(1, n_v):
        t_hop(t).wait_recv()
        src = (v + n_v - t) % n_v
        got = arecv[src]
        e = got[:, ch - 128:].astype(jnp.float32)[I_DEV * Q - 1:I_DEV * Q, 127:128]
        cyc_out[src] = decode(got, e)

    for s in range(1, n_o):
        src = (o + s) % n_o
        for b in range(per_owner):
            pltpu.make_async_remote_copy(
                src_ref=ls.at[0], dst_ref=lr.at[src, b], send_sem=l_send.at[0],
                recv_sem=l_recv.at[src, b], device_id=(o, v), device_id_type=MESH,
            ).wait_recv()
            got = lr[src, b]
            e = got[:, NVP - 128:].astype(jnp.float32)[0:1, 127:128]
            lad_out[b] = lad_out[b] + decode(got, e)

    for d in range(nz):
        for c in range(depth):
            if d < nz - 1:
                @pl.when((z - d >= 0) & (z + 1 < nz))
                def _():
                    up_hop(d, c).wait_send()

                @pl.when((z + d < nz) & (z >= 1))
                def _():
                    down_hop(d, c).wait_send()
            if d == 0:
                for h in x_hops(0, z, c):
                    h.wait_send()
            else:
                @pl.when(z - d >= 0)
                def _():
                    for h in x_hops(d, z - d, c):
                        h.wait_send()

                @pl.when(z + d < nz)
                def _():
                    for h in x_hops(nz - 1 + d, z + d, c):
                        h.wait_send()
    for s in range(1, n_o):
        c_hop(s).wait_send()
    for t in range(1, n_v):
        t_hop(t).wait_send()

    def sent(slot, _):
        @pl.when(slot // per_owner != o)
        def _():
            l_hop(slot).wait_send()

        return 0

    lax.fori_loop(0, n_v, sent, 0)


def irrep_of(blocks, index):
    bounds = jnp.cumsum(blocks)[:-1]
    return jnp.sum((index[:, None] >= bounds[None, :]).astype(jnp.int32), axis=1)


def shards(
    amplitudes,
    ladder_ints,
    cycle_amps,
    cycle_ints,
    occ_blocks,
    virt_blocks,
    occ_start,
    virt_start,
    eps_occ,
    eps_virt,
):
    n_o, n_v = lax.axis_size("opair"), lax.axis_size("vpair")
    a_win = A_DEV * n_v
    pairs, depth = amplitudes.shape[:2]
    pairs_pad = up_to(pairs, 16)
    jb = cycle_ints.shape[2]
    jb_pad = up_to(jb + 1, 128)
    ch = up_to((jb_pad + Q) // Q, 128)
    rows = a_win * I_DEV
    per_owner = n_v // n_o
    nx = row_length(n_v)
    nz = n_v // nx

    amps = jnp.pad(amplitudes.transpose(1, 0, 2), ((0, 0), (0, pairs_pad - pairs), (0, 0)))
    ints = ladder_ints.reshape(depth, NV, NV)
    w = cycle_amps.reshape(depth, NO, n_o, I_DEV, a_win).transpose(0, 2, 4, 3, 1).reshape(depth, n_o * rows, NO)
    dma = pltpu.SemaphoreType.DMA
    lad, cyc = pl.pallas_call(
        functools.partial(kernel, n_o, n_v, pairs, pairs_pad, depth, jb, jb_pad, ch, a_win),
        out_shape=(
            jax.ShapeDtypeStruct((per_owner, pairs_pad, NVP), jnp.float32),
            jax.ShapeDtypeStruct((n_v, I_DEV * Q, ch), jnp.float32),
        ),
        in_specs=[
            pl.BlockSpec(memory_space=pl.ANY),
            pl.BlockSpec(memory_space=pl.ANY),
            pl.BlockSpec(memory_space=pltpu.VMEM),
            pl.BlockSpec(memory_space=pl.ANY),
        ],
        out_specs=[pl.BlockSpec(memory_space=pltpu.VMEM)] * 2,
        scratch_shapes=[
            pltpu.VMEM((n_v, depth, pairs_pad, NV), jnp.bfloat16),
            pltpu.VMEM((depth, NV, NV), jnp.bfloat16),
            pltpu.VMEM((depth, NO, jb), jnp.bfloat16),
            pltpu.VMEM((n_o * rows, jb_pad), jnp.float32),
            pltpu.VMEM((n_o - 1, rows, jb_pad), jnp.int16),
            pltpu.VMEM((n_o - 1, rows, jb_pad), jnp.int16),
            pltpu.VMEM((rows, Q * ch), jnp.float32),
            pltpu.VMEM((n_v, I_DEV * Q, ch), jnp.float32),
            pltpu.VMEM((n_v, I_DEV * Q, ch), jnp.int16),
            pltpu.VMEM((n_v, I_DEV * Q, ch), jnp.int16),
            pltpu.VMEM((pairs_pad, NVP), jnp.float32),
            pltpu.VMEM((n_v, pairs_pad, NVP), jnp.int16),
            pltpu.VMEM((n_o, per_owner, pairs_pad, NVP), jnp.int16),
            dma((3,)),
            dma((n_v, depth)),
            dma((nz, depth)),
            dma((nz, depth)),
            dma((2 * nz - 1, max(nx - 1, 1), depth)),
            dma((n_o - 1,)),
            dma((n_o - 1,)),
            dma((n_v - 1,)),
            dma((n_v - 1,)),
            dma((n_v,)),
            dma((n_o, per_owner)),
        ],
        compiler_params=pltpu.CompilerParams(
            collective_id=0, has_side_effects=True, vmem_limit_bytes=58 * 1024 * 1024
        ),
        cost_estimate=pl.CostEstimate(
            flops=2 * n_v * pairs * depth * NV * NV + 2 * n_o * rows * depth * NO * jb,
            bytes_accessed=2 * depth * (NV * NV + NO * jb), transcendentals=0,
        ),
        name="residual",
    )(amps, ints, w, cycle_ints)
    ladder = lad[:, :pairs, :NV].reshape(I_DEV, A_DEV, NO, NV)
    cycle = cyc.reshape(n_v, I_DEV, Q * ch)[:, :, :jb].transpose(1, 0, 2).reshape(I_DEV, A_DEV, NO, NV)
    resid = ladder + cycle
    first_occ = occ_start[0] + lax.axis_index("opair") * I_DEV
    first_virt = virt_start[0] + lax.axis_index("vpair") * A_DEV
    glob_i = first_occ + jnp.arange(I_DEV, dtype=jnp.int32)
    glob_a = first_virt + jnp.arange(A_DEV, dtype=jnp.int32)
    sym_i = irrep_of(occ_blocks, glob_i)
    sym_a = irrep_of(virt_blocks, glob_a)
    sym_j = irrep_of(occ_blocks, jnp.arange(NO, dtype=jnp.int32))
    sym_b = irrep_of(virt_blocks, jnp.arange(NV, dtype=jnp.int32))
    total_sym = jnp.bitwise_xor(
        jnp.bitwise_xor(sym_i[:, None, None, None], sym_a[None, :, None, None]),
        jnp.bitwise_xor(sym_j[None, None, :, None], sym_b[None, None, None, :]),
    )
    e_i = lax.dynamic_slice_in_dim(eps_occ, first_occ, I_DEV)
    e_a = lax.dynamic_slice_in_dim(eps_virt, first_virt, A_DEV)
    denom = (
        e_i[:, None, None, None]
        - e_a[None, :, None, None]
        + eps_occ[None, None, :, None]
        - eps_virt[None, None, None, :]
    )
    return jnp.where(total_sym == 0, resid / denom, jnp.float32(0.0))


def solution(mesh):
    placed = (
        P("vpair", "opair", None),
        P("opair", None, "vpair", None),
        P("opair", None, None),
        P("opair", None, "vpair"),
        P(),
        P(),
        P(),
        P(),
        P(),
        P(),
    )
    return jax.shard_map(
        shards,
        mesh=mesh,
        in_specs=placed,
        out_specs=P("opair", "vpair", None, None),
        check_vma=False,
    )
```

```python
import functools

import jax
import jax.numpy as jnp
from jax import lax
from jax.experimental import pallas as pl
from jax.experimental.pallas import tpu as pltpu
from jax.sharding import PartitionSpec as P

NO = 100
NV = 1000
I_DEV = 2
A_DEV = 1
NVP = 1024
Q = 8
FULL = 32000.0
MESH = pl.DeviceIdType.MESH


def up_to(n, m):
    return (n + m - 1) // m * m


def row_length(n_v):
    x = 1
    while (2 * x) * (2 * x) * 2 <= n_v and n_v % (2 * x) == 0:
        x *= 2
    return x


def exponent(x):
    top = jnp.max(jnp.max(jnp.abs(x), axis=1, keepdims=True), axis=0, keepdims=True)
    return jnp.floor(jnp.log(jnp.maximum(top, 1e-30)) * 1.4426950408889634) + 1.0


def code(x, e, is_scale):
    q = jnp.round(x * (FULL * jnp.exp2(-e)))
    return jnp.where(is_scale, e, q).astype(jnp.int32).astype(jnp.int16)


def decode(q, e):
    return q.astype(jnp.float32) * (jnp.exp2(e) * (1.0 / FULL))


def kernel(
    n_o, n_v, pairs, pairs_pad, depth, jb, jb_pad, ch, a_win,
    amps, ints, w_ref, cyc_ints, lad_out, cyc_out,
    a_buf, gat, rest, rest_sum, b_buf, y_buf, part, cs, cr, total, tile, asend, arecv, acc, ls, lr,
    copy_sem, a_recv, up_send, down_send, x_send, cross_send, c_send, c_recv, t_send, t_recv, l_send, l_recv,
):
    o = lax.axis_index("opair")
    v = lax.axis_index("vpair")
    nx = row_length(n_v)
    nz = n_v // nx
    z, x = v // nx, v % nx
    rows = a_win * I_DEV
    per_owner = n_v // n_o
    base = pairs // 16 * 16
    left = pairs - base
    pieces = depth + 1

    b_copy = pltpu.make_async_copy(ints, b_buf, copy_sem.at[0])
    y_copy = pltpu.make_async_copy(cyc_ints, y_buf, copy_sem.at[1])
    own_copy = pltpu.make_async_copy(amps, a_buf, copy_sem.at[2])
    own_copy.start()
    y_copy.start()
    b_copy.start()

    barrier = pltpu.get_barrier_semaphore()
    for t in range(1, n_v):
        pl.semaphore_signal(barrier, inc=1, device_id=(o, (v + t) % n_v), device_id_type=MESH)
    for s in range(1, n_o):
        pl.semaphore_signal(barrier, inc=1, device_id=((o + s) % n_o, v), device_id_type=MESH)
    rest_sum[...] = jnp.zeros_like(rest_sum)
    own_copy.wait()
    for c in range(depth):
        rest_sum[0, c * left:(c + 1) * left, 0:NV] = a_buf[c, base:pairs, :].astype(jnp.float32)
    rest[v] = rest_sum[0, :, 0:NV].astype(jnp.bfloat16)
    pl.semaphore_wait(barrier, n_v - 1 + n_o - 1)

    def piece(slot, c):
        return gat.at[slot, c] if c < depth else rest.at[slot]

    def hop(src, slot, c, send, to):
        return pltpu.make_async_remote_copy(
            src_ref=src, dst_ref=piece(slot, c), send_sem=send, recv_sem=a_recv.at[slot, c],
            device_id=(o, to), device_id_type=MESH,
        )

    def block_src(slot, c, own):
        return a_buf.at[c, pl.ds(0, base)] if own and c < depth else piece(slot, c)

    def up_hop(d, c):
        slot = (z - d) * nx + x
        return hop(block_src(slot, c, d == 0), slot, c, up_send.at[d, c], v + nx)

    def down_hop(d, c):
        slot = (z + d) * nx + x
        return hop(block_src(slot, c, d == 0), slot, c, down_send.at[d, c], v - nx)

    def x_hops(k, zb, c):
        if (k == 1 or k == nz) and c == depth - 1:
            return []
        slot = zb * nx + x
        return [
            hop(block_src(slot, c, k == 0), slot, c, x_send.at[k, t - 1, c], z * nx + (x + t) % nx)
            for t in range(1, nx)
        ]

    def cross(k, t):
        slot = z * nx + (x + t) % nx
        c = depth - 1
        return hop(gat.at[slot, c], slot, c, cross_send.at[k, t - 1], v + nx if k == 0 else v - nx)

    def arrived(slot, c):
        pltpu.make_async_remote_copy(
            src_ref=piece(slot, c), dst_ref=piece(slot, c), send_sem=copy_sem.at[0],
            recv_sem=a_recv.at[slot, c], device_id=(o, v), device_id_type=MESH,
        ).wait_recv()

    for c in range(pieces):
        if nz > 1:
            @pl.when(z + 1 < nz)
            def _():
                up_hop(0, c).start()

            @pl.when(z >= 1)
            def _():
                down_hop(0, c).start()
        for h in x_hops(0, z, c):
            h.start()

    acc[...] = jnp.zeros_like(acc)
    part[:, jb_pad - 128:] = jnp.zeros((part.shape[0], 128), jnp.float32)
    y_copy.wait()
    step = 14 * 128
    for at in range(0, jb, step):
        end = min(at + step, jb)
        sum_c = None
        for c in range(depth):
            term = jnp.dot(w_ref[c], y_buf[c, :, at:end], preferred_element_type=jnp.float32)
            sum_c = term if sum_c is None else sum_c + term
        part[:, at:end] = sum_c

    is_scale_c = lax.broadcasted_iota(jnp.int32, (rows, jb_pad), 1) == jb_pad - 1

    def c_hop(s):
        return pltpu.make_async_remote_copy(
            src_ref=cs.at[s - 1], dst_ref=cr.at[s - 1], send_sem=c_send.at[s - 1],
            recv_sem=c_recv.at[s - 1], device_id=((o + s) % n_o, v), device_id_type=MESH,
        )

    for s in range(1, n_o):
        to = (o + s) % n_o
        block = part[pl.ds(pl.multiple_of(to * rows, rows), rows), :]
        cs[s - 1] = code(block, exponent(block), is_scale_c)
        c_hop(s).start()

    col = lax.broadcasted_iota(jnp.int32, (pairs_pad, NVP), 1)

    def l_hop(slot):
        owner = slot // per_owner
        return pltpu.make_async_remote_copy(
            src_ref=ls.at[slot], dst_ref=lr.at[o, slot % per_owner], send_sem=l_send.at[slot],
            recv_sem=l_recv.at[o, slot % per_owner], device_id=(owner, v), device_id_type=MESH,
        )

    def multiply(slot):
        for at in range(0, NV, 256):
            end = min(at + 256, NV)
            sum_c = None
            for c in range(depth):
                lhs = jnp.concatenate([gat[slot, c], rest[slot]], axis=0)
                term = jnp.dot(lhs, b_buf[c, :, at:end], preferred_element_type=jnp.float32)
                rest_sum[c, :, at:end] = term[base:]
                sum_c = term[:base] if sum_c is None else sum_c + term[:base]
            acc[0:base, at:end] = sum_c
        end_sum = rest_sum[0, 0:left, :]
        for c in range(1, depth):
            end_sum = end_sum + rest_sum[c, c * left:(c + 1) * left, :]
        acc[base:pairs, :] = end_sum

        @pl.when(slot // per_owner == o)
        def _():
            lad_out[slot % per_owner] = acc[...]

        @pl.when(slot // per_owner != o)
        def _():
            block = acc[...]
            ls[slot] = code(block, exponent(block), col >= NV)
            l_hop(slot).start()

    def take_row(zb):
        def one(t, _):
            slot = zb * nx + (x + t) % nx
            for c in range(pieces):
                arrived(slot, c)
            multiply(slot)
            return 0

        lax.fori_loop(1, nx, one, 0)

    b_copy.wait()
    for c in range(depth):
        gat[v, c] = a_buf[c, 0:base, :]
    multiply(v)

    def t_hop(t):
        to = (v + t) % n_v
        return pltpu.make_async_remote_copy(
            src_ref=asend.at[to], dst_ref=arecv.at[v], send_sem=t_send.at[t - 1],
            recv_sem=t_recv.at[t - 1], device_id=(o, to), device_id_type=MESH,
        )

    def cycle_exchange():
        sum_o = part[pl.ds(pl.multiple_of(o * rows, rows), rows), :]
        for s in range(1, n_o):
            c_hop(s).wait_recv()
            got = cr[s - 1]
            e = got[rows - 1:rows, jb_pad - 128:].astype(jnp.float32)[:, 127:128]
            sum_o = sum_o + jnp.where(is_scale_c, 0.0, decode(got, e))
        total[:, 0:jb_pad] = sum_o
        total[:, jb_pad:] = jnp.zeros((rows, Q * ch - jb_pad), jnp.float32)
        spot = (lax.broadcasted_iota(jnp.int32, (I_DEV * Q, ch), 0) == I_DEV * Q - 1) & (
            lax.broadcasted_iota(jnp.int32, (I_DEV * Q, ch), 1) == ch - 1
        )

        def one(t, _):
            a = (v + t) % n_v
            for i in range(I_DEV):
                for q in range(Q):
                    tile[a, i * Q + q:i * Q + q + 1, :] = total[pl.ds(i * a_win + a, 1), q * ch:q * ch + ch]
            block = tile[a]
            asend[a] = code(block, exponent(block), spot)
            return 0

        lax.fori_loop(0, n_v, one, 0)
        for t in range(1, n_v):
            t_hop(t).start()

    for d in range(1, nz):
        for c in range(pieces):
            @pl.when(z - d >= 0)
            def _():
                arrived((z - d) * nx + x, c)

                @pl.when(z + 1 < nz)
                def _():
                    up_hop(d, c).start()

                for h in x_hops(d, z - d, c):
                    h.start()

            @pl.when(z + d < nz)
            def _():
                arrived((z + d) * nx + x, c)

                @pl.when(z >= 1)
                def _():
                    down_hop(d, c).start()

                for h in x_hops(nz - 1 + d, z + d, c):
                    h.start()

        if d == min(2, nz - 1):
            cycle_exchange()
        if d == 1:
            for t in range(1, nx):
                arrived(z * nx + (x + t) % nx, depth - 1)

                @pl.when(z + 1 < nz)
                def _():
                    cross(0, t).start()

                @pl.when(z >= 1)
                def _():
                    cross(1, t).start()

            def one(t, _):
                slot = z * nx + (x + t) % nx
                for c in range(pieces):
                    if c != depth - 1:
                        arrived(slot, c)
                multiply(slot)
                return 0

            lax.fori_loop(1, nx, one, 0)
        else:
            @pl.when(z - (d - 1) >= 0)
            def _():
                take_row(z - (d - 1))

            @pl.when(z + (d - 1) < nz)
            def _():
                take_row(z + (d - 1))

        @pl.when(z - d >= 0)
        def _():
            multiply((z - d) * nx + x)

        @pl.when(z + d < nz)
        def _():
            multiply((z + d) * nx + x)

    @pl.when(z - (nz - 1) >= 0)
    def _():
        take_row(z - (nz - 1))

    @pl.when(z + (nz - 1) < nz)
    def _():
        take_row(z + (nz - 1))

    cyc_out[v] = tile[v]
    for t in range(1, n_v):
        t_hop(t).wait_recv()
        src = (v + n_v - t) % n_v
        got = arecv[src]
        e = got[:, ch - 128:].astype(jnp.float32)[I_DEV * Q - 1:I_DEV * Q, 127:128]
        cyc_out[src] = decode(got, e)

    for s in range(1, n_o):
        src = (o + s) % n_o
        for b in range(per_owner):
            pltpu.make_async_remote_copy(
                src_ref=ls.at[0], dst_ref=lr.at[src, b], send_sem=l_send.at[0],
                recv_sem=l_recv.at[src, b], device_id=(o, v), device_id_type=MESH,
            ).wait_recv()
            got = lr[src, b]
            e = got[:, NVP - 128:].astype(jnp.float32)[0:1, 127:128]
            lad_out[b] = lad_out[b] + decode(got, e)

    for d in range(nz):
        for c in range(pieces):
            if d < nz - 1:
                @pl.when((z - d >= 0) & (z + 1 < nz))
                def _():
                    up_hop(d, c).wait_send()

                @pl.when((z + d < nz) & (z >= 1))
                def _():
                    down_hop(d, c).wait_send()
            if d == 0:
                for h in x_hops(0, z, c):
                    h.wait_send()
            else:
                @pl.when(z - d >= 0)
                def _():
                    for h in x_hops(d, z - d, c):
                        h.wait_send()

                @pl.when(z + d < nz)
                def _():
                    for h in x_hops(nz - 1 + d, z + d, c):
                        h.wait_send()
    for t in range(1, nx):
        @pl.when(z + 1 < nz)
        def _():
            cross(0, t).wait_send()

        @pl.when(z >= 1)
        def _():
            cross(1, t).wait_send()

    for s in range(1, n_o):
        c_hop(s).wait_send()
    for t in range(1, n_v):
        t_hop(t).wait_send()

    def sent(slot, _):
        @pl.when(slot // per_owner != o)
        def _():
            l_hop(slot).wait_send()

        return 0

    lax.fori_loop(0, n_v, sent, 0)


def irrep_of(blocks, index):
    bounds = jnp.cumsum(blocks)[:-1]
    return jnp.sum((index[:, None] >= bounds[None, :]).astype(jnp.int32), axis=1)


def shards(
    amplitudes,
    ladder_ints,
    cycle_amps,
    cycle_ints,
    occ_blocks,
    virt_blocks,
    occ_start,
    virt_start,
    eps_occ,
    eps_virt,
):
    n_o, n_v = lax.axis_size("opair"), lax.axis_size("vpair")
    a_win = A_DEV * n_v
    pairs, depth = amplitudes.shape[:2]
    pairs_pad = up_to(pairs, 16)
    jb = cycle_ints.shape[2]
    jb_pad = up_to(jb + 1, 128)
    ch = up_to((jb_pad + Q) // Q, 128)
    rows = a_win * I_DEV
    per_owner = n_v // n_o
    nx = row_length(n_v)
    nz = n_v // nx

    amps = amplitudes.transpose(1, 0, 2)
    base = pairs // 16 * 16
    short = up_to(depth * (pairs - base), 16)
    ints = ladder_ints.reshape(depth, NV, NV)
    w = cycle_amps.transpose(0, 2, 1)
    dma = pltpu.SemaphoreType.DMA
    lad, cyc = pl.pallas_call(
        functools.partial(kernel, n_o, n_v, pairs, pairs_pad, depth, jb, jb_pad, ch, a_win),
        out_shape=(
            jax.ShapeDtypeStruct((per_owner, pairs_pad, NVP), jnp.float32),
            jax.ShapeDtypeStruct((n_v, I_DEV * Q, ch), jnp.float32),
        ),
        in_specs=[
            pl.BlockSpec(memory_space=pl.ANY),
            pl.BlockSpec(memory_space=pl.ANY),
            pl.BlockSpec(memory_space=pltpu.VMEM),
            pl.BlockSpec(memory_space=pl.ANY),
        ],
        out_specs=[pl.BlockSpec(memory_space=pltpu.VMEM)] * 2,
        scratch_shapes=[
            pltpu.VMEM((depth, pairs, NV), jnp.bfloat16),
            pltpu.VMEM((n_v, depth, base, NV), jnp.bfloat16),
            pltpu.VMEM((n_v, short, NV), jnp.bfloat16),
            pltpu.VMEM((depth, short, NVP), jnp.float32),
            pltpu.VMEM((depth, NV, NV), jnp.bfloat16),
            pltpu.VMEM((depth, NO, jb), jnp.bfloat16),
            pltpu.VMEM((n_o * rows, jb_pad), jnp.float32),
            pltpu.VMEM((n_o - 1, rows, jb_pad), jnp.int16),
            pltpu.VMEM((n_o - 1, rows, jb_pad), jnp.int16),
            pltpu.VMEM((rows, Q * ch), jnp.float32),
            pltpu.VMEM((n_v, I_DEV * Q, ch), jnp.float32),
            pltpu.VMEM((n_v, I_DEV * Q, ch), jnp.int16),
            pltpu.VMEM((n_v, I_DEV * Q, ch), jnp.int16),
            pltpu.VMEM((pairs_pad, NVP), jnp.float32),
            pltpu.VMEM((n_v, pairs_pad, NVP), jnp.int16),
            pltpu.VMEM((n_o, per_owner, pairs_pad, NVP), jnp.int16),
            dma((3,)),
            dma((n_v, depth + 1)),
            dma((nz, depth + 1)),
            dma((nz, depth + 1)),
            dma((2 * nz - 1, max(nx - 1, 1), depth + 1)),
            dma((2, max(nx - 1, 1))),
            dma((n_o - 1,)),
            dma((n_o - 1,)),
            dma((n_v - 1,)),
            dma((n_v - 1,)),
            dma((n_v,)),
            dma((n_o, per_owner)),
        ],
        compiler_params=pltpu.CompilerParams(
            collective_id=0, has_side_effects=True, vmem_limit_bytes=58 * 1024 * 1024
        ),
        cost_estimate=pl.CostEstimate(
            flops=2 * n_v * pairs * depth * NV * NV + 2 * n_o * rows * depth * NO * jb,
            bytes_accessed=2 * depth * (NV * NV + NO * jb), transcendentals=0,
        ),
        name="residual",
    )(amps, ints, w, cycle_ints)
    ladder = lad[:, :pairs, :NV].reshape(I_DEV, A_DEV, NO, NV)
    cycle = cyc.reshape(n_v, I_DEV, Q * ch)[:, :, :jb].transpose(1, 0, 2).reshape(I_DEV, A_DEV, NO, NV)
    resid = ladder + cycle
    first_occ = occ_start[0] + lax.axis_index("opair") * I_DEV
    first_virt = virt_start[0] + lax.axis_index("vpair") * A_DEV
    glob_i = first_occ + jnp.arange(I_DEV, dtype=jnp.int32)
    glob_a = first_virt + jnp.arange(A_DEV, dtype=jnp.int32)
    sym_i = irrep_of(occ_blocks, glob_i)
    sym_a = irrep_of(virt_blocks, glob_a)
    sym_j = irrep_of(occ_blocks, jnp.arange(NO, dtype=jnp.int32))
    sym_b = irrep_of(virt_blocks, jnp.arange(NV, dtype=jnp.int32))
    total_sym = jnp.bitwise_xor(
        jnp.bitwise_xor(sym_i[:, None, None, None], sym_a[None, :, None, None]),
        jnp.bitwise_xor(sym_j[None, None, :, None], sym_b[None, None, None, :]),
    )
    e_i = lax.dynamic_slice_in_dim(eps_occ, first_occ, I_DEV)
    e_a = lax.dynamic_slice_in_dim(eps_virt, first_virt, A_DEV)
    denom = (
        e_i[:, None, None, None]
        - e_a[None, :, None, None]
        + eps_occ[None, None, :, None]
        - eps_virt[None, None, None, :]
    )
    return jnp.where(total_sym == 0, resid / denom, jnp.float32(0.0))


def solution(mesh):
    placed = (
        P("vpair", "opair", None),
        P("opair", None, "vpair", None),
        P("opair", None, None),
        P("opair", None, "vpair"),
        P(),
        P(),
        P(),
        P(),
        P(),
        P(),
    )
    return jax.shard_map(
        shards,
        mesh=mesh,
        in_specs=placed,
        out_specs=P("opair", "vpair", None, None),
        check_vma=False,
    )
```

```python
import functools

import jax
import jax.numpy as jnp
from jax import lax
from jax.experimental import pallas as pl
from jax.experimental.pallas import tpu as pltpu
from jax.sharding import PartitionSpec as P

NO = 100
NV = 1000
I_DEV = 2
A_DEV = 1
NVP = 1024
Q = 8
FULL = 32000.0
MESH = pl.DeviceIdType.MESH


def up_to(n, m):
    return (n + m - 1) // m * m


def row_length(n_v):
    x = 1
    while (2 * x) * (2 * x) * 2 <= n_v and n_v % (2 * x) == 0:
        x *= 2
    return x


def exponent(x):
    top = jnp.max(jnp.max(jnp.abs(x), axis=1, keepdims=True), axis=0, keepdims=True)
    return jnp.floor(jnp.log(jnp.maximum(top, 1e-30)) * 1.4426950408889634) + 1.0


def code(x, e, is_scale):
    q = jnp.round(x * (FULL * jnp.exp2(-e)))
    return jnp.where(is_scale, e, q).astype(jnp.int32).astype(jnp.int16)


def decode(q, e):
    return q.astype(jnp.float32) * (jnp.exp2(e) * (1.0 / FULL))


def kernel(
    n_o, n_v, pairs, pairs_pad, depth, jb, jb_pad, ch, a_win,
    amps, ints, w_ref, cyc_ints, lad_out, cyc_out,
    a_buf, gat, rest, rest_sum, b_buf, y_buf, part, cs, cr, total, tile, asend, arecv, acc, ls, lr,
    copy_sem, a_recv, up_send, down_send, x_send, cross_send, c_send, c_recv, t_send, t_recv, l_send, l_recv,
):
    o = lax.axis_index("opair")
    v = lax.axis_index("vpair")
    nx = row_length(n_v)
    nz = n_v // nx
    z, x = v // nx, v % nx
    rows = a_win * I_DEV
    per_owner = n_v // n_o
    base = pairs // 16 * 16
    left = pairs - base
    pieces = depth + 1

    b_copy = pltpu.make_async_copy(ints, b_buf, copy_sem.at[0])
    y_copy = pltpu.make_async_copy(cyc_ints, y_buf, copy_sem.at[1])
    own_copy = pltpu.make_async_copy(amps, a_buf, copy_sem.at[2])
    own_copy.start()
    y_copy.start()
    b_copy.start()

    barrier = pltpu.get_barrier_semaphore()
    for t in range(1, n_v):
        pl.semaphore_signal(barrier, inc=1, device_id=(o, (v + t) % n_v), device_id_type=MESH)
    for s in range(1, n_o):
        pl.semaphore_signal(barrier, inc=1, device_id=((o + s) % n_o, v), device_id_type=MESH)
    rest_sum[...] = jnp.zeros_like(rest_sum)
    own_copy.wait()
    for c in range(depth):
        rest_sum[0, c * left:(c + 1) * left, 0:NV] = a_buf[c, base:pairs, :].astype(jnp.float32)
    rest[v] = rest_sum[0, :, 0:NV].astype(jnp.bfloat16)
    pl.semaphore_wait(barrier, n_v - 1 + n_o - 1)

    def piece(slot, c):
        return gat.at[slot, c] if c < depth else rest.at[slot]

    def hop(src, slot, c, send, to):
        return pltpu.make_async_remote_copy(
            src_ref=src, dst_ref=piece(slot, c), send_sem=send, recv_sem=a_recv.at[slot, c],
            device_id=(o, to), device_id_type=MESH,
        )

    def block_src(slot, c, own):
        return a_buf.at[c, pl.ds(0, base)] if own and c < depth else piece(slot, c)

    def up_hop(d, c):
        slot = (z - d) * nx + x
        return hop(block_src(slot, c, d == 0), slot, c, up_send.at[d, c], v + nx)

    def down_hop(d, c):
        slot = (z + d) * nx + x
        return hop(block_src(slot, c, d == 0), slot, c, down_send.at[d, c], v - nx)

    def x_hops(k, zb, c):
        if (k == 1 or k == nz) and c == depth - 1:
            return []
        slot = zb * nx + x
        return [
            hop(block_src(slot, c, k == 0), slot, c, x_send.at[k, t - 1, c], z * nx + (x + t) % nx)
            for t in range(1, nx)
        ]

    def cross(k, t):
        slot = z * nx + (x + t) % nx
        c = depth - 1
        return hop(gat.at[slot, c], slot, c, cross_send.at[k, t - 1], v + nx if k == 0 else v - nx)

    def arrived(slot, c):
        pltpu.make_async_remote_copy(
            src_ref=piece(slot, c), dst_ref=piece(slot, c), send_sem=copy_sem.at[0],
            recv_sem=a_recv.at[slot, c], device_id=(o, v), device_id_type=MESH,
        ).wait_recv()

    for c in range(pieces):
        if nz > 1:
            @pl.when(z + 1 < nz)
            def _():
                up_hop(0, c).start()

            @pl.when(z >= 1)
            def _():
                down_hop(0, c).start()
        for h in x_hops(0, z, c):
            h.start()

    acc[...] = jnp.zeros_like(acc)
    part[:, jb_pad - 128:] = jnp.zeros((part.shape[0], 128), jnp.float32)
    y_copy.wait()
    step = 14 * 128
    for at in range(0, jb, step):
        end = min(at + step, jb)
        sum_c = None
        for c in range(depth):
            term = jnp.dot(w_ref[c], y_buf[c, :, at:end], preferred_element_type=jnp.float32)
            sum_c = term if sum_c is None else sum_c + term
        part[:, at:end] = sum_c

    is_scale_c = lax.broadcasted_iota(jnp.int32, (rows, jb_pad), 1) == jb_pad - 1

    def c_hop(s):
        return pltpu.make_async_remote_copy(
            src_ref=cs.at[s - 1], dst_ref=cr.at[s - 1], send_sem=c_send.at[s - 1],
            recv_sem=c_recv.at[s - 1], device_id=((o + s) % n_o, v), device_id_type=MESH,
        )

    for s in range(1, n_o):
        to = (o + s) % n_o
        block = part[pl.ds(pl.multiple_of(to * rows, rows), rows), :]
        cs[s - 1] = code(block, exponent(block), is_scale_c)
        c_hop(s).start()

    col = lax.broadcasted_iota(jnp.int32, (pairs_pad, NVP), 1)

    def l_hop(slot):
        owner = slot // per_owner
        return pltpu.make_async_remote_copy(
            src_ref=ls.at[slot], dst_ref=lr.at[o, slot % per_owner], send_sem=l_send.at[slot],
            recv_sem=l_recv.at[o, slot % per_owner], device_id=(owner, v), device_id_type=MESH,
        )

    def multiply(slot):
        for at in range(0, NV, 256):
            end = min(at + 256, NV)
            sum_c = None
            for c in range(depth):
                lhs = jnp.concatenate([gat[slot, c], rest[slot]], axis=0)
                term = jnp.dot(lhs, b_buf[c, :, at:end], preferred_element_type=jnp.float32)
                rest_sum[c, :, at:end] = term[base:]
                sum_c = term[:base] if sum_c is None else sum_c + term[:base]
            acc[0:base, at:end] = sum_c
        end_sum = rest_sum[0, 0:left, :]
        for c in range(1, depth):
            end_sum = end_sum + rest_sum[c, c * left:(c + 1) * left, :]
        acc[base:pairs, :] = end_sum

        @pl.when(slot // per_owner == o)
        def _():
            lad_out[slot % per_owner] = acc[...]

        @pl.when(slot // per_owner != o)
        def _():
            block = acc[...]
            ls[slot] = code(block, exponent(block), col >= NV)
            l_hop(slot).start()

    def take_row(zb):
        def one(t, _):
            slot = zb * nx + (x + t) % nx
            for c in range(pieces):
                arrived(slot, c)
            multiply(slot)
            return 0

        lax.fori_loop(1, nx, one, 0)

    b_copy.wait()
    for c in range(depth):
        gat[v, c] = a_buf[c, 0:base, :]

    def t_hop(t):
        to = (v + t) % n_v
        return pltpu.make_async_remote_copy(
            src_ref=asend.at[to], dst_ref=arecv.at[v], send_sem=t_send.at[t - 1],
            recv_sem=t_recv.at[t - 1], device_id=(o, to), device_id_type=MESH,
        )

    def cycle_exchange():
        sum_o = part[pl.ds(pl.multiple_of(o * rows, rows), rows), :]
        for s in range(1, n_o):
            c_hop(s).wait_recv()
            got = cr[s - 1]
            e = got[rows - 1:rows, jb_pad - 128:].astype(jnp.float32)[:, 127:128]
            sum_o = sum_o + jnp.where(is_scale_c, 0.0, decode(got, e))
        total[:, 0:jb_pad] = sum_o
        total[:, jb_pad:] = jnp.zeros((rows, Q * ch - jb_pad), jnp.float32)
        spot = (lax.broadcasted_iota(jnp.int32, (I_DEV * Q, ch), 0) == I_DEV * Q - 1) & (
            lax.broadcasted_iota(jnp.int32, (I_DEV * Q, ch), 1) == ch - 1
        )

        def one(t, _):
            a = (v + t) % n_v
            for i in range(I_DEV):
                for q in range(Q):
                    tile[a, i * Q + q:i * Q + q + 1, :] = total[pl.ds(i * a_win + a, 1), q * ch:q * ch + ch]
            block = tile[a]
            asend[a] = code(block, exponent(block), spot)
            return 0

        lax.fori_loop(0, n_v, one, 0)
        for t in range(1, n_v):
            t_hop(t).start()

    for d in range(1, nz):
        for c in range(pieces):
            @pl.when(z - d >= 0)
            def _():
                arrived((z - d) * nx + x, c)

                @pl.when(z + 1 < nz)
                def _():
                    up_hop(d, c).start()

                for h in x_hops(d, z - d, c):
                    h.start()

            @pl.when(z + d < nz)
            def _():
                arrived((z + d) * nx + x, c)

                @pl.when(z >= 1)
                def _():
                    down_hop(d, c).start()

                for h in x_hops(nz - 1 + d, z + d, c):
                    h.start()

            if d == 1:
                if c == 0:
                    multiply(v)
            else:
                back = d - 1

                @pl.when((z - back >= 0) if c % 2 == 0 else (z + back < nz))
                def _():
                    zb = z - back if c % 2 == 0 else z + back
                    if c < 2:
                        multiply(zb * nx + x)
                    elif c < 4:
                        take_row(zb)

        if d == min(2, nz - 1):
            cycle_exchange()
        if d == 1:
            for t in range(1, nx):
                arrived(z * nx + (x + t) % nx, depth - 1)

                @pl.when(z + 1 < nz)
                def _():
                    cross(0, t).start()

                @pl.when(z >= 1)
                def _():
                    cross(1, t).start()

            def one(t, _):
                slot = z * nx + (x + t) % nx
                for c in range(pieces):
                    if c != depth - 1:
                        arrived(slot, c)
                multiply(slot)
                return 0

            lax.fori_loop(1, nx, one, 0)

    far = nz - 1

    @pl.when(z - far >= 0)
    def _():
        multiply((z - far) * nx + x)

    @pl.when(z + far < nz)
    def _():
        multiply((z + far) * nx + x)

    cyc_out[v] = tile[v]
    for t in range(1, n_v):
        t_hop(t).wait_recv()
        src = (v + n_v - t) % n_v
        got = arecv[src]
        e = got[:, ch - 128:].astype(jnp.float32)[I_DEV * Q - 1:I_DEV * Q, 127:128]
        cyc_out[src] = decode(got, e)

    @pl.when(z - far >= 0)
    def _():
        take_row(z - far)

    @pl.when(z + far < nz)
    def _():
        take_row(z + far)

    for s in range(1, n_o):
        src = (o + s) % n_o
        for b in range(per_owner):
            pltpu.make_async_remote_copy(
                src_ref=ls.at[0], dst_ref=lr.at[src, b], send_sem=l_send.at[0],
                recv_sem=l_recv.at[src, b], device_id=(o, v), device_id_type=MESH,
            ).wait_recv()
            got = lr[src, b]
            e = got[:, NVP - 128:].astype(jnp.float32)[0:1, 127:128]
            lad_out[b] = lad_out[b] + decode(got, e)

    for d in range(nz):
        for c in range(pieces):
            if d < nz - 1:
                @pl.when((z - d >= 0) & (z + 1 < nz))
                def _():
                    up_hop(d, c).wait_send()

                @pl.when((z + d < nz) & (z >= 1))
                def _():
                    down_hop(d, c).wait_send()
            if d == 0:
                for h in x_hops(0, z, c):
                    h.wait_send()
            else:
                @pl.when(z - d >= 0)
                def _():
                    for h in x_hops(d, z - d, c):
                        h.wait_send()

                @pl.when(z + d < nz)
                def _():
                    for h in x_hops(nz - 1 + d, z + d, c):
                        h.wait_send()
    for t in range(1, nx):
        @pl.when(z + 1 < nz)
        def _():
            cross(0, t).wait_send()

        @pl.when(z >= 1)
        def _():
            cross(1, t).wait_send()

    for s in range(1, n_o):
        c_hop(s).wait_send()
    for t in range(1, n_v):
        t_hop(t).wait_send()

    def sent(slot, _):
        @pl.when(slot // per_owner != o)
        def _():
            l_hop(slot).wait_send()

        return 0

    lax.fori_loop(0, n_v, sent, 0)


def irrep_of(blocks, index):
    bounds = jnp.cumsum(blocks)[:-1]
    return jnp.sum((index[:, None] >= bounds[None, :]).astype(jnp.int32), axis=1)


def shards(
    amplitudes,
    ladder_ints,
    cycle_amps,
    cycle_ints,
    occ_blocks,
    virt_blocks,
    occ_start,
    virt_start,
    eps_occ,
    eps_virt,
):
    n_o, n_v = lax.axis_size("opair"), lax.axis_size("vpair")
    a_win = A_DEV * n_v
    pairs, depth = amplitudes.shape[:2]
    pairs_pad = up_to(pairs, 16)
    jb = cycle_ints.shape[2]
    jb_pad = up_to(jb + 1, 128)
    ch = up_to((jb_pad + Q) // Q, 128)
    rows = a_win * I_DEV
    per_owner = n_v // n_o
    nx = row_length(n_v)
    nz = n_v // nx

    amps = amplitudes.transpose(1, 0, 2)
    base = pairs // 16 * 16
    short = up_to(depth * (pairs - base), 16)
    ints = ladder_ints.reshape(depth, NV, NV)
    w = cycle_amps.transpose(0, 2, 1)
    dma = pltpu.SemaphoreType.DMA
    lad, cyc = pl.pallas_call(
        functools.partial(kernel, n_o, n_v, pairs, pairs_pad, depth, jb, jb_pad, ch, a_win),
        out_shape=(
            jax.ShapeDtypeStruct((per_owner, pairs_pad, NVP), jnp.float32),
            jax.ShapeDtypeStruct((n_v, I_DEV * Q, ch), jnp.float32),
        ),
        in_specs=[
            pl.BlockSpec(memory_space=pl.ANY),
            pl.BlockSpec(memory_space=pl.ANY),
            pl.BlockSpec(memory_space=pltpu.VMEM),
            pl.BlockSpec(memory_space=pl.ANY),
        ],
        out_specs=[pl.BlockSpec(memory_space=pltpu.VMEM)] * 2,
        scratch_shapes=[
            pltpu.VMEM((depth, pairs, NV), jnp.bfloat16),
            pltpu.VMEM((n_v, depth, base, NV), jnp.bfloat16),
            pltpu.VMEM((n_v, short, NV), jnp.bfloat16),
            pltpu.VMEM((depth, short, NVP), jnp.float32),
            pltpu.VMEM((depth, NV, NV), jnp.bfloat16),
            pltpu.VMEM((depth, NO, jb), jnp.bfloat16),
            pltpu.VMEM((n_o * rows, jb_pad), jnp.float32),
            pltpu.VMEM((n_o - 1, rows, jb_pad), jnp.int16),
            pltpu.VMEM((n_o - 1, rows, jb_pad), jnp.int16),
            pltpu.VMEM((rows, Q * ch), jnp.float32),
            pltpu.VMEM((n_v, I_DEV * Q, ch), jnp.float32),
            pltpu.VMEM((n_v, I_DEV * Q, ch), jnp.int16),
            pltpu.VMEM((n_v, I_DEV * Q, ch), jnp.int16),
            pltpu.VMEM((pairs_pad, NVP), jnp.float32),
            pltpu.VMEM((n_v, pairs_pad, NVP), jnp.int16),
            pltpu.VMEM((n_o, per_owner, pairs_pad, NVP), jnp.int16),
            dma((3,)),
            dma((n_v, depth + 1)),
            dma((nz, depth + 1)),
            dma((nz, depth + 1)),
            dma((2 * nz - 1, max(nx - 1, 1), depth + 1)),
            dma((2, max(nx - 1, 1))),
            dma((n_o - 1,)),
            dma((n_o - 1,)),
            dma((n_v - 1,)),
            dma((n_v - 1,)),
            dma((n_v,)),
            dma((n_o, per_owner)),
        ],
        compiler_params=pltpu.CompilerParams(
            collective_id=0, has_side_effects=True, vmem_limit_bytes=58 * 1024 * 1024
        ),
        cost_estimate=pl.CostEstimate(
            flops=2 * n_v * pairs * depth * NV * NV + 2 * n_o * rows * depth * NO * jb,
            bytes_accessed=2 * depth * (NV * NV + NO * jb), transcendentals=0,
        ),
        name="residual",
    )(amps, ints, w, cycle_ints)
    ladder = lad[:, :pairs, :NV].reshape(I_DEV, A_DEV, NO, NV)
    cycle = cyc.reshape(n_v, I_DEV, Q * ch)[:, :, :jb].transpose(1, 0, 2).reshape(I_DEV, A_DEV, NO, NV)
    resid = ladder + cycle
    first_occ = occ_start[0] + lax.axis_index("opair") * I_DEV
    first_virt = virt_start[0] + lax.axis_index("vpair") * A_DEV
    glob_i = first_occ + jnp.arange(I_DEV, dtype=jnp.int32)
    glob_a = first_virt + jnp.arange(A_DEV, dtype=jnp.int32)
    sym_i = irrep_of(occ_blocks, glob_i)
    sym_a = irrep_of(virt_blocks, glob_a)
    sym_j = irrep_of(occ_blocks, jnp.arange(NO, dtype=jnp.int32))
    sym_b = irrep_of(virt_blocks, jnp.arange(NV, dtype=jnp.int32))
    total_sym = jnp.bitwise_xor(
        jnp.bitwise_xor(sym_i[:, None, None, None], sym_a[None, :, None, None]),
        jnp.bitwise_xor(sym_j[None, None, :, None], sym_b[None, None, None, :]),
    )
    e_i = lax.dynamic_slice_in_dim(eps_occ, first_occ, I_DEV)
    e_a = lax.dynamic_slice_in_dim(eps_virt, first_virt, A_DEV)
    denom = (
        e_i[:, None, None, None]
        - e_a[None, :, None, None]
        + eps_occ[None, None, :, None]
        - eps_virt[None, None, None, :]
    )
    return jnp.where(total_sym == 0, resid / denom, jnp.float32(0.0))


def solution(mesh):
    placed = (
        P("vpair", "opair", None),
        P("opair", None, "vpair", None),
        P("opair", None, None),
        P("opair", None, "vpair"),
        P(),
        P(),
        P(),
        P(),
        P(),
        P(),
    )
    return jax.shard_map(
        shards,
        mesh=mesh,
        in_specs=placed,
        out_specs=P("opair", "vpair", None, None),
        check_vma=False,
    )
```

```python
import functools

import jax
import jax.numpy as jnp
from jax import lax
from jax.experimental import pallas as pl
from jax.experimental.pallas import tpu as pltpu
from jax.sharding import PartitionSpec as P

NO = 100
NV = 1000
I_DEV = 2
A_DEV = 1
NVP = 1024
Q = 8
FULL = 32000.0
MESH = pl.DeviceIdType.MESH


def up_to(n, m):
    return (n + m - 1) // m * m


def row_length(n_v):
    x = 1
    while (2 * x) * (2 * x) * 2 <= n_v and n_v % (2 * x) == 0:
        x *= 2
    return x


def exponent(x):
    top = jnp.max(jnp.max(jnp.abs(x), axis=1, keepdims=True), axis=0, keepdims=True)
    return jnp.floor(jnp.log(jnp.maximum(top, 1e-30)) * 1.4426950408889634) + 1.0


def code(x, e, is_scale):
    q = jnp.round(x * (FULL * jnp.exp2(-e)))
    return jnp.where(is_scale, e, q).astype(jnp.int32).astype(jnp.int16)


def decode(q, e):
    return q.astype(jnp.float32) * (jnp.exp2(e) * (1.0 / FULL))


def kernel(
    n_o, n_v, pairs, pairs_pad, depth, jb, jb_pad, ch, a_win,
    amps, ints, w_ref, cyc_ints, lad_out, cyc_out,
    a_buf, gat, rest, rest_sum, b_buf, y_buf, part, cs, cr, total, tile, asend, arecv, acc, ls, lr,
    copy_sem, a_recv, up_send, down_send, x_send, cross_send, c_send, c_recv, t_send, t_recv, l_send, l_recv,
):
    o = lax.axis_index("opair")
    v = lax.axis_index("vpair")
    nx = row_length(n_v)
    nz = n_v // nx
    z, x = v // nx, v % nx
    rows = a_win * I_DEV
    per_owner = n_v // n_o
    base = pairs // 16 * 16
    left = pairs - base
    pieces = depth + 1

    b_copy = pltpu.make_async_copy(ints, b_buf, copy_sem.at[0])
    y_copy = pltpu.make_async_copy(cyc_ints, y_buf, copy_sem.at[1])
    own_copy = pltpu.make_async_copy(amps, a_buf, copy_sem.at[2])
    own_copy.start()
    y_copy.start()
    b_copy.start()

    barrier = pltpu.get_barrier_semaphore()
    for t in range(1, n_v):
        pl.semaphore_signal(barrier, inc=1, device_id=(o, (v + t) % n_v), device_id_type=MESH)
    for s in range(1, n_o):
        pl.semaphore_signal(barrier, inc=1, device_id=((o + s) % n_o, v), device_id_type=MESH)
    rest_sum[...] = jnp.zeros_like(rest_sum)
    own_copy.wait()
    for c in range(depth):
        rest_sum[0, c * left:(c + 1) * left, 0:NV] = a_buf[c, base:pairs, :].astype(jnp.float32)
    rest[v] = rest_sum[0, :, 0:NV].astype(jnp.bfloat16)
    pl.semaphore_wait(barrier, n_v - 1 + n_o - 1)

    def piece(slot, c):
        return gat.at[slot, c] if c < depth else rest.at[slot]

    def hop(src, slot, c, send, to):
        return pltpu.make_async_remote_copy(
            src_ref=src, dst_ref=piece(slot, c), send_sem=send, recv_sem=a_recv.at[slot, c],
            device_id=(o, to), device_id_type=MESH,
        )

    def block_src(slot, c, own):
        return a_buf.at[c, pl.ds(0, base)] if own and c < depth else piece(slot, c)

    def up_hop(d, c):
        slot = (z - d) * nx + x
        return hop(block_src(slot, c, d == 0), slot, c, up_send.at[d, c], v + nx)

    def down_hop(d, c):
        slot = (z + d) * nx + x
        return hop(block_src(slot, c, d == 0), slot, c, down_send.at[d, c], v - nx)

    def x_hops(k, zb, c):
        if (k == 1 or k == nz) and c == depth - 1:
            return []
        slot = zb * nx + x
        return [
            hop(block_src(slot, c, k == 0), slot, c, x_send.at[k, t - 1, c], z * nx + (x + t) % nx)
            for t in range(1, nx)
        ]

    def cross(k, t):
        slot = z * nx + (x + t) % nx
        c = depth - 1
        return hop(gat.at[slot, c], slot, c, cross_send.at[k, t - 1], v + nx if k == 0 else v - nx)

    def arrived(slot, c):
        pltpu.make_async_remote_copy(
            src_ref=piece(slot, c), dst_ref=piece(slot, c), send_sem=copy_sem.at[0],
            recv_sem=a_recv.at[slot, c], device_id=(o, v), device_id_type=MESH,
        ).wait_recv()

    for c in range(pieces):
        if nz > 1:
            @pl.when(z + 1 < nz)
            def _():
                up_hop(0, c).start()

            @pl.when(z >= 1)
            def _():
                down_hop(0, c).start()
        for h in x_hops(0, z, c):
            h.start()

    acc[...] = jnp.zeros_like(acc)
    part[:, jb_pad - 128:] = jnp.zeros((part.shape[0], 128), jnp.float32)
    y_copy.wait()
    step = 14 * 128
    for at in range(0, jb, step):
        end = min(at + step, jb)
        sum_c = None
        for c in range(depth):
            term = jnp.dot(w_ref[c], y_buf[c, :, at:end], preferred_element_type=jnp.float32)
            sum_c = term if sum_c is None else sum_c + term
        part[:, at:end] = sum_c

    is_scale_c = lax.broadcasted_iota(jnp.int32, (rows, jb_pad), 1) == jb_pad - 1

    def c_hop(s):
        return pltpu.make_async_remote_copy(
            src_ref=cs.at[s - 1], dst_ref=cr.at[s - 1], send_sem=c_send.at[s - 1],
            recv_sem=c_recv.at[s - 1], device_id=((o + s) % n_o, v), device_id_type=MESH,
        )

    for s in range(1, n_o):
        to = (o + s) % n_o
        block = part[pl.ds(pl.multiple_of(to * rows, rows), rows), :]
        cs[s - 1] = code(block, exponent(block), is_scale_c)
        c_hop(s).start()

    col = lax.broadcasted_iota(jnp.int32, (pairs_pad, NVP), 1)

    def l_hop(slot):
        owner = slot // per_owner
        return pltpu.make_async_remote_copy(
            src_ref=ls.at[slot], dst_ref=lr.at[o, slot % per_owner], send_sem=l_send.at[slot],
            recv_sem=l_recv.at[o, slot % per_owner], device_id=(owner, v), device_id_type=MESH,
        )

    def multiply(slot):
        for at in range(0, NV, 256):
            end = min(at + 256, NV)
            sum_c = None
            for c in range(depth):
                lhs = jnp.concatenate([gat[slot, c], rest[slot]], axis=0)
                term = jnp.dot(lhs, b_buf[c, :, at:end], preferred_element_type=jnp.float32)
                rest_sum[c, :, at:end] = term[base:]
                sum_c = term[:base] if sum_c is None else sum_c + term[:base]
            acc[0:base, at:end] = sum_c
        end_sum = rest_sum[0, 0:left, :]
        for c in range(1, depth):
            end_sum = end_sum + rest_sum[c, c * left:(c + 1) * left, :]
        acc[base:pairs, :] = end_sum

        @pl.when(slot // per_owner == o)
        def _():
            lad_out[slot % per_owner] = acc[...]

        @pl.when(slot // per_owner != o)
        def _():
            block = acc[...]
            ls[slot] = code(block, exponent(block), col >= NV)
            l_hop(slot).start()

    def take_row(zb):
        def one(t, _):
            slot = zb * nx + (x + t) % nx
            for c in range(pieces):
                arrived(slot, c)
            multiply(slot)
            return 0

        lax.fori_loop(1, nx, one, 0)

    b_copy.wait()
    for c in range(depth):
        gat[v, c] = a_buf[c, 0:base, :]
    multiply(v)

    def t_hop(t):
        to = (v + t) % n_v
        return pltpu.make_async_remote_copy(
            src_ref=asend.at[to], dst_ref=arecv.at[v], send_sem=t_send.at[t - 1],
            recv_sem=t_recv.at[t - 1], device_id=(o, to), device_id_type=MESH,
        )

    def cycle_exchange():
        sum_o = part[pl.ds(pl.multiple_of(o * rows, rows), rows), :]
        for s in range(1, n_o):
            c_hop(s).wait_recv()
            got = cr[s - 1]
            e = got[rows - 1:rows, jb_pad - 128:].astype(jnp.float32)[:, 127:128]
            sum_o = sum_o + jnp.where(is_scale_c, 0.0, decode(got, e))
        total[:, 0:jb_pad] = sum_o
        total[:, jb_pad:] = jnp.zeros((rows, Q * ch - jb_pad), jnp.float32)
        spot = (lax.broadcasted_iota(jnp.int32, (I_DEV * Q, ch), 0) == I_DEV * Q - 1) & (
            lax.broadcasted_iota(jnp.int32, (I_DEV * Q, ch), 1) == ch - 1
        )

        def one(t, _):
            a = (v + t) % n_v
            for i in range(I_DEV):
                for q in range(Q):
                    tile[a, i * Q + q:i * Q + q + 1, :] = total[pl.ds(i * a_win + a, 1), q * ch:q * ch + ch]
            block = tile[a]
            asend[a] = code(block, exponent(block), spot)
            return 0

        lax.fori_loop(0, n_v, one, 0)
        for t in range(1, n_v):
            t_hop(t).start()

    for d in range(1, nz):
        for c in range(pieces):
            @pl.when(z - d >= 0)
            def _():
                arrived((z - d) * nx + x, c)

                @pl.when(z + 1 < nz)
                def _():
                    up_hop(d, c).start()

                for h in x_hops(d, z - d, c):
                    h.start()

            @pl.when(z + d < nz)
            def _():
                arrived((z + d) * nx + x, c)

                @pl.when(z >= 1)
                def _():
                    down_hop(d, c).start()

                for h in x_hops(nz - 1 + d, z + d, c):
                    h.start()

        if d == min(2, nz - 1):
            cycle_exchange()
        if d == 1:
            for t in range(1, nx):
                arrived(z * nx + (x + t) % nx, depth - 1)

                @pl.when(z + 1 < nz)
                def _():
                    cross(0, t).start()

                @pl.when(z >= 1)
                def _():
                    cross(1, t).start()

            def one(t, _):
                slot = z * nx + (x + t) % nx
                for c in range(pieces):
                    if c != depth - 1:
                        arrived(slot, c)
                multiply(slot)
                return 0

            lax.fori_loop(1, nx, one, 0)
        else:
            @pl.when(z - (d - 1) >= 0)
            def _():
                take_row(z - (d - 1))

            @pl.when(z + (d - 1) < nz)
            def _():
                take_row(z + (d - 1))

        @pl.when(z - d >= 0)
        def _():
            multiply((z - d) * nx + x)

        @pl.when(z + d < nz)
        def _():
            multiply((z + d) * nx + x)

    @pl.when(z - (nz - 1) >= 0)
    def _():
        take_row(z - (nz - 1))

    @pl.when(z + (nz - 1) < nz)
    def _():
        take_row(z + (nz - 1))

    cyc_out[v] = tile[v]
    for t in range(1, n_v):
        t_hop(t).wait_recv()
        src = (v + n_v - t) % n_v
        got = arecv[src]
        e = got[:, ch - 128:].astype(jnp.float32)[I_DEV * Q - 1:I_DEV * Q, 127:128]
        cyc_out[src] = decode(got, e)

    for s in range(1, n_o):
        src = (o + s) % n_o
        for b in range(per_owner):
            pltpu.make_async_remote_copy(
                src_ref=ls.at[0], dst_ref=lr.at[src, b], send_sem=l_send.at[0],
                recv_sem=l_recv.at[src, b], device_id=(o, v), device_id_type=MESH,
            ).wait_recv()
            got = lr[src, b]
            e = got[:, NVP - 128:].astype(jnp.float32)[0:1, 127:128]
            lad_out[b] = lad_out[b] + decode(got, e)

    for d in range(nz):
        for c in range(pieces):
            if d < nz - 1:
                @pl.when((z - d >= 0) & (z + 1 < nz))
                def _():
                    up_hop(d, c).wait_send()

                @pl.when((z + d < nz) & (z >= 1))
                def _():
                    down_hop(d, c).wait_send()
            if d == 0:
                for h in x_hops(0, z, c):
                    h.wait_send()
            else:
                @pl.when(z - d >= 0)
                def _():
                    for h in x_hops(d, z - d, c):
                        h.wait_send()

                @pl.when(z + d < nz)
                def _():
                    for h in x_hops(nz - 1 + d, z + d, c):
                        h.wait_send()
    for t in range(1, nx):
        @pl.when(z + 1 < nz)
        def _():
            cross(0, t).wait_send()

        @pl.when(z >= 1)
        def _():
            cross(1, t).wait_send()

    for s in range(1, n_o):
        c_hop(s).wait_send()
    for t in range(1, n_v):
        t_hop(t).wait_send()

    def sent(slot, _):
        @pl.when(slot // per_owner != o)
        def _():
            l_hop(slot).wait_send()

        return 0

    lax.fori_loop(0, n_v, sent, 0)


def picked(values, index):
    here = index[:, None] == jnp.arange(values.shape[0], dtype=jnp.int32)[None, :]
    return jnp.sum(jnp.where(here, values[None, :], 0.0), axis=1)


def irrep_of(blocks, index):
    bounds = jnp.sum(jnp.where(jnp.tri(7, 8, dtype=jnp.bool_), blocks[None, :], 0), axis=1)
    return jnp.sum((index[:, None] >= bounds[None, :]).astype(jnp.int32), axis=1)


def shards(
    amplitudes,
    ladder_ints,
    cycle_amps,
    cycle_ints,
    occ_blocks,
    virt_blocks,
    occ_start,
    virt_start,
    eps_occ,
    eps_virt,
):
    n_o, n_v = lax.axis_size("opair"), lax.axis_size("vpair")
    a_win = A_DEV * n_v
    pairs, depth = amplitudes.shape[:2]
    pairs_pad = up_to(pairs, 16)
    jb = cycle_ints.shape[2]
    jb_pad = up_to(jb + 1, 128)
    ch = up_to((jb_pad + Q) // Q, 128)
    rows = a_win * I_DEV
    per_owner = n_v // n_o
    nx = row_length(n_v)
    nz = n_v // nx

    amps = amplitudes.transpose(1, 0, 2)
    base = pairs // 16 * 16
    short = up_to(depth * (pairs - base), 16)
    ints = ladder_ints.reshape(depth, NV, NV)
    w = cycle_amps.transpose(0, 2, 1)
    dma = pltpu.SemaphoreType.DMA
    lad, cyc = pl.pallas_call(
        functools.partial(kernel, n_o, n_v, pairs, pairs_pad, depth, jb, jb_pad, ch, a_win),
        out_shape=(
            jax.ShapeDtypeStruct((per_owner, pairs_pad, NVP), jnp.float32),
            jax.ShapeDtypeStruct((n_v, I_DEV * Q, ch), jnp.float32),
        ),
        in_specs=[
            pl.BlockSpec(memory_space=pl.ANY),
            pl.BlockSpec(memory_space=pl.ANY),
            pl.BlockSpec(memory_space=pltpu.VMEM),
            pl.BlockSpec(memory_space=pl.ANY),
        ],
        out_specs=[pl.BlockSpec(memory_space=pltpu.VMEM)] * 2,
        scratch_shapes=[
            pltpu.VMEM((depth, pairs, NV), jnp.bfloat16),
            pltpu.VMEM((n_v, depth, base, NV), jnp.bfloat16),
            pltpu.VMEM((n_v, short, NV), jnp.bfloat16),
            pltpu.VMEM((depth, short, NVP), jnp.float32),
            pltpu.VMEM((depth, NV, NV), jnp.bfloat16),
            pltpu.VMEM((depth, NO, jb), jnp.bfloat16),
            pltpu.VMEM((n_o * rows, jb_pad), jnp.float32),
            pltpu.VMEM((n_o - 1, rows, jb_pad), jnp.int16),
            pltpu.VMEM((n_o - 1, rows, jb_pad), jnp.int16),
            pltpu.VMEM((rows, Q * ch), jnp.float32),
            pltpu.VMEM((n_v, I_DEV * Q, ch), jnp.float32),
            pltpu.VMEM((n_v, I_DEV * Q, ch), jnp.int16),
            pltpu.VMEM((n_v, I_DEV * Q, ch), jnp.int16),
            pltpu.VMEM((pairs_pad, NVP), jnp.float32),
            pltpu.VMEM((n_v, pairs_pad, NVP), jnp.int16),
            pltpu.VMEM((n_o, per_owner, pairs_pad, NVP), jnp.int16),
            dma((3,)),
            dma((n_v, depth + 1)),
            dma((nz, depth + 1)),
            dma((nz, depth + 1)),
            dma((2 * nz - 1, max(nx - 1, 1), depth + 1)),
            dma((2, max(nx - 1, 1))),
            dma((n_o - 1,)),
            dma((n_o - 1,)),
            dma((n_v - 1,)),
            dma((n_v - 1,)),
            dma((n_v,)),
            dma((n_o, per_owner)),
        ],
        compiler_params=pltpu.CompilerParams(
            collective_id=0, has_side_effects=True, vmem_limit_bytes=58 * 1024 * 1024
        ),
        cost_estimate=pl.CostEstimate(
            flops=2 * n_v * pairs * depth * NV * NV + 2 * n_o * rows * depth * NO * jb,
            bytes_accessed=2 * depth * (NV * NV + NO * jb), transcendentals=0,
        ),
        name="residual",
    )(amps, ints, w, cycle_ints)
    ladder = lad[:, :pairs, :NV].reshape(I_DEV, A_DEV, NO, NV)
    cycle = cyc.reshape(n_v, I_DEV, Q * ch)[:, :, :jb].transpose(1, 0, 2).reshape(I_DEV, A_DEV, NO, NV)
    resid = ladder + cycle
    first_occ = occ_start[0] + lax.axis_index("opair") * I_DEV
    first_virt = virt_start[0] + lax.axis_index("vpair") * A_DEV
    glob_i = first_occ + jnp.arange(I_DEV, dtype=jnp.int32)
    glob_a = first_virt + jnp.arange(A_DEV, dtype=jnp.int32)
    sym_i = irrep_of(occ_blocks, glob_i)
    sym_a = irrep_of(virt_blocks, glob_a)
    sym_j = irrep_of(occ_blocks, jnp.arange(NO, dtype=jnp.int32))
    sym_b = irrep_of(virt_blocks, jnp.arange(NV, dtype=jnp.int32))
    total_sym = jnp.bitwise_xor(
        jnp.bitwise_xor(sym_i[:, None, None, None], sym_a[None, :, None, None]),
        jnp.bitwise_xor(sym_j[None, None, :, None], sym_b[None, None, None, :]),
    )
    e_i = picked(eps_occ, glob_i)
    e_a = picked(eps_virt, glob_a)
    denom = (
        e_i[:, None, None, None]
        - e_a[None, :, None, None]
        + eps_occ[None, None, :, None]
        - eps_virt[None, None, None, :]
    )
    return jnp.where(total_sym == 0, resid / denom, jnp.float32(0.0))


def solution(mesh):
    placed = (
        P("vpair", "opair", None),
        P("opair", None, "vpair", None),
        P("opair", None, None),
        P("opair", None, "vpair"),
        P(),
        P(),
        P(),
        P(),
        P(),
        P(),
    )
    return jax.shard_map(
        shards,
        mesh=mesh,
        in_specs=placed,
        out_specs=P("opair", "vpair", None, None),
        check_vma=False,
    )
```
